128 devices in a mesh: inst: 32 (over y_hi, z, x), tp: 4 (over y_lo, core).
Axes of the slice: x: 4, y: 4 (y_hi: 2, y_lo: 2; y = y_hi * 2 + y_lo), z: 4, core: 2. Of those that a mesh axis runs over, the one named last changes fastest.
Arguments:
- gate_param: float32 [3072, 1280], P(('inst', 'tp')), may hold values from -0.15625 to 0.15625
- gate_grad: float32 [3072, 1280], P(('inst', 'tp')), may hold values from -6 to 6
- gate_m: float32 [3072, 1280], P(('inst', 'tp')), may hold values from -4 to 4
- gate_v: float32 [3072, 1280], P(('inst', 'tp')), may hold values from 0.1 to 3
- down_param: float32 [1280, 3072], P(('inst', 'tp')), may hold values from -0.109375 to 0.109375
- down_grad: float32 [1280, 3072], P(('inst', 'tp')), may hold values from -6 to 6
- down_m: float32 [1280, 3072], P(('inst', 'tp')), may hold values from -4 to 4
- down_v: float32 [1280, 3072], P(('inst', 'tp')), may hold values from 0.1 to 3
Outputs:
- gate_param_new: float32 [3072, 1280], P(('inst', 'tp'))
- gate_m_new: float32 [3072, 1280], P(('inst', 'tp'))
- gate_v_new: float32 [3072, 1280], P(('inst', 'tp'))
- down_param_new: float32 [1280, 3072], P(('inst', 'tp'))
- down_m_new: float32 [1280, 3072], P(('inst', 'tp'))
- down_v_new: float32 [1280, 3072], P(('inst', 'tp'))
- gate_quant: bfloat16 [32, 3072, 1280], P('inst', 'tp')
- gate_scale: float32 [32, 24, 10], P('inst', 'tp')
- down_quant: bfloat16 [32, 1280, 3072], P('inst', None, 'tp')
- down_scale: float32 [32, 10, 24], P('inst', None, 'tp')
The draws below stay inside these ranges and needn't reach their ends.
All inputs are finite; a program needn't handle non-finite values. Where the reference program divides by a largest or mean magnitude, that divisor is 1e-20 or more.
Results may differ from the reference program's by a relative error of at most 0.001.
Values may be sent and summed in bfloat16 or wider, within the bound.
No kernel may reach another device: no remote copies, remote signals or barrier semaphores. Data moves between devices by JAX's collectives and lax.ppermute only.
A program may use at most 128 MiB of HBM per device.

```python
import math
import jax
import jax.numpy as jnp
from jax import lax

D = 1280
FF = 3072
BLOCK = 128
N_INST = 32


def level_of(own_key, dims, split, least, high):
    def one(axis_at, parts):
        steps = jax.random.uniform(jax.random.fold_in(jax.random.fold_in(own_key, 6), axis_at), (parts,), jnp.float32, least / len(split), high / len(split))
        return jnp.repeat(jnp.exp(steps), dims[axis_at] // parts).reshape((-1,) + (1,) * (len(dims) - axis_at - 1))

    factor_of = one(*split[0])
    for cut in split[1:]:
        factor_of = factor_of * one(*cut)
    return factor_of


def gaussian(key, shape, deviation, bound, cuts=(), held_as=jnp.bfloat16):
    result = deviation * jax.random.normal(key, shape, jnp.float32)
    if cuts:
        result = result * level_of(key, shape, cuts, -0.22, 0.18)
    return jnp.clip(result, -bound, bound).astype(held_as)


def setup_inputs(seed: int = 0) -> dict:
    streams_of = jax.random.split(jax.random.key(seed), 9)
    gate_param = gaussian(streams_of[0], (FF, D), D ** -0.5, 0.15625, ((0, 128),), jnp.float32)
    gate_grad = gaussian(streams_of[1], (FF, D), 1.0, 6.0, ((0, 128),), jnp.float32)
    gate_m = gaussian(streams_of[2], (FF, D), 0.3, 4.0, ((0, 128),), jnp.float32)
    gate_v = jnp.clip(jnp.exp(math.log(3.0) - 3.4011974 * jax.random.uniform(streams_of[3], (FF, D), jnp.float32) ** level_of(streams_of[3], (FF, D), ((0, 128),), -0.2, 0.2)), 0.1, 3.0)
    down_param = gaussian(streams_of[4], (D, FF), FF ** -0.5, 0.109375, ((0, 128),), jnp.float32)
    down_grad = gaussian(streams_of[5], (D, FF), 1.0, 6.0, ((0, 128),), jnp.float32)
    down_m = gaussian(streams_of[6], (D, FF), 0.3, 4.0, ((0, 128),), jnp.float32)
    down_v = jnp.clip(jnp.exp(math.log(3.0) - 3.4011974 * jax.random.uniform(streams_of[7], (D, FF), jnp.float32) ** level_of(streams_of[7], (D, FF), ((0, 128),), -0.2, 0.2)), 0.1, 3.0)
    return {"gate_param": gate_param, "gate_grad": gate_grad, "gate_m": gate_m, "gate_v": gate_v, "down_param": down_param, "down_grad": down_grad, "down_m": down_m, "down_v": down_v}


beta_one = 0.9
beta_two = 0.999
adam_eps = 1e-08
step_rate = 0.02
decay_rate = 0.1
correct_one = 0.9999734386011124
correct_two = 0.09520785288629038
scale_eps = 1e-06

def adamw_step(param, grad, moment, second):
    moment_new = beta_one * moment + (1.0 - beta_one) * grad
    second_new = beta_two * second + (1.0 - beta_two) * grad * grad
    update = moment_new / correct_one / (jnp.sqrt(second_new / correct_two) + adam_eps)
    param_new = param - step_rate * (update + decay_rate * param)
    return (param_new, moment_new, second_new)

def quantize(weight):
    row_count, col_count = weight.shape
    blocks = weight.reshape(row_count // BLOCK, BLOCK, col_count // BLOCK, BLOCK)
    block_max = lax.optimization_barrier(jnp.max(jnp.abs(blocks), axis=(1, 3))) + scale_eps
    coded = (blocks / block_max[:, None, :, None]).reshape(row_count, col_count).astype(jnp.bfloat16)
    return (coded, block_max)

def replicas(array):
    return jnp.broadcast_to(array[None], (N_INST,) + array.shape)

def reference(gate_param, gate_grad, gate_m, gate_v, down_param, down_grad, down_m, down_v):
    gate_new, gate_m_new, gate_v_new = adamw_step(gate_param, gate_grad, gate_m, gate_v)
    down_new, down_m_new, down_v_new = adamw_step(down_param, down_grad, down_m, down_v)
    gate_quant, gate_scale = quantize(gate_new)
    down_quant, down_scale = quantize(down_new)
    return (gate_new, gate_m_new, gate_v_new, down_new, down_m_new, down_v_new, replicas(gate_quant), replicas(gate_scale), replicas(down_quant), replicas(down_scale))
```

```python
import jax
import jax.numpy as jnp
from jax import lax
from jax.experimental import pallas as pl
from jax.experimental.pallas import tpu as pltpu
from jax.sharding import Mesh, PartitionSpec as P

BLOCK = 128
LANES = 128
AXES = ("yh", "z", "x", "yl", "c")
SIZES = (2, 4, 4, 2, 2)
ROWS = ("yh", "z", "x", "yl", "c")
INST = ("yh", "z", "x")
TP = ("yl", "c")

beta_one = 0.9
beta_two = 0.999
adam_eps = 1e-08
step_rate = 0.02
decay_rate = 0.1
correct_one = 0.9999734386011124
correct_two = 0.09520785288629038
scale_eps = 1e-06

GATE_ROWS = 24
GATE_COLS = 1280
DOWN_ROWS = 10
DOWN_COLS = 3072
SHARE = 768
GATE_BLOCKS = GATE_COLS // BLOCK
DOWN_BLOCKS = SHARE // BLOCK
DOWN_LANE = 64


def index_of(yh, z, x, yl, c):
    return (((yh * 4 + z) * 4 + x) * 2 + yl) * 2 + c


def vmem():
    return pl.BlockSpec(memory_space=pltpu.VMEM)


def anywhere():
    return pl.BlockSpec(memory_space=pl.ANY)


def adamw_step(param, grad, moment, second):
    moment_new = beta_one * moment + (1.0 - beta_one) * grad
    second_new = beta_two * second + (1.0 - beta_two) * grad * grad
    update = moment_new / correct_one / (jnp.sqrt(second_new / correct_two) + adam_eps)
    param_new = param - step_rate * (update + decay_rate * param)
    return (param_new, moment_new, second_new)


def adam_kernel(gp, gg, gm, gv, dp, dg, dm, dv, gpo, gmo, gvo, dpo, dmo, dvo, slots):
    gpo[...], gmo[...], gvo[...] = adamw_step(gp[...], gg[...], gm[...], gv[...])
    down, dmo[...], dvo[...] = adamw_step(dp[...], dg[...], dm[...], dv[...])
    dpo[...] = down
    for rank in range(4):
        for k in range(DOWN_BLOCKS):
            col = rank * SHARE + k * BLOCK
            for half in range(2):
                slots[half * 4 + rank, 8 * k : 8 * k + 8, :] = down[0:8, col : col + BLOCK]
                slots[half * 4 + rank, 48 + 2 * k : 50 + 2 * k, :] = down[8:10, col : col + BLOCK]
        for half in range(2):
            slots[half * 4 + rank, 60:64, :] = jnp.zeros((4, LANES), jnp.float32)


def adam(gate, down):
    gate_shape = jax.ShapeDtypeStruct((GATE_ROWS, GATE_COLS), jnp.float32)
    down_shape = jax.ShapeDtypeStruct((DOWN_ROWS, DOWN_COLS), jnp.float32)
    return pl.pallas_call(
        adam_kernel,
        out_shape=(gate_shape,) * 3
        + (down_shape,) * 3
        + (jax.ShapeDtypeStruct((8, 64, LANES), jnp.float32),),
        in_specs=[vmem()] * 8,
        out_specs=(vmem(),) * 7,
    )(*gate, *down)


def block_maxima(rows, first, row_count, blocks):
    size = jnp.abs(rows)
    below = lax.broadcasted_iota(jnp.int32, (row_count, 1), 0) < first
    out = []
    for part in (jnp.where(below, size, 0.0), jnp.where(below, 0.0, size)):
        top = jnp.max(part, axis=0, keepdims=True)
        tall = jnp.concatenate([top[:, k * BLOCK : (k + 1) * BLOCK] for k in range(blocks)], axis=0)
        out.append(jnp.max(tall, axis=1, keepdims=True))
    return out


def maxima_kernel(g0, g1, slots, gate, down, maxima):
    c_lane = lax.broadcasted_iota(jnp.int32, (1, LANES), 1)
    z, x = lax.axis_index("z"), lax.axis_index("x")
    yh = lax.axis_index("yh")
    own = pl.multiple_of(yh * GATE_ROWS, 8)
    other = pl.multiple_of((1 - yh) * GATE_ROWS, 8)
    gate[pl.ds(own, GATE_ROWS), :] = g0[...]
    gate[pl.ds(other, GATE_ROWS), :] = g1[...]
    for h in range(2):
        for s in range(4):
            at = h * 40 + s * DOWN_ROWS
            for k in range(DOWN_BLOCKS):
                col = slice(k * BLOCK, (k + 1) * BLOCK)
                down[at : at + 8, col] = slots[h * 4 + s, 8 * k : 8 * k + 8, :]
                down[at + 8 : at + 10, col] = slots[h * 4 + s, 48 + 2 * k : 50 + 2 * k, :]
    zl, yl = z % 2, z // 2
    at = x * 96 + yl * 48
    blk = at // BLOCK
    low, high = block_maxima(gate[...], (blk + 1) * BLOCK - at, 48, GATE_BLOCKS)
    lane = blk + 3 * zl
    top = jnp.where(c_lane == lane, low, 0.0) + jnp.where(c_lane == lane + 1, high, 0.0)
    maxima[0:GATE_BLOCKS, :] = top
    maxima[GATE_BLOCKS:16, :] = jnp.zeros((16 - GATE_BLOCKS, LANES), jnp.float32)
    at = z * 160 + x * 40
    blk = at // BLOCK
    for h in range(2):
        low, high = block_maxima(down[h * 40 : h * 40 + 40, :], (blk + 1) * BLOCK - at, 40, DOWN_BLOCKS)
        lane = DOWN_LANE + 5 * h + blk
        maxima[0:DOWN_BLOCKS, :] = (
            maxima[0:DOWN_BLOCKS, :]
            + jnp.where(c_lane == lane, low, 0.0)
            + jnp.where(c_lane == lane + 1, high, 0.0)
        )


def partial_maxima(g0, g1, slots):
    return pl.pallas_call(
        maxima_kernel,
        out_shape=(
            jax.ShapeDtypeStruct((48, GATE_COLS), jnp.float32),
            jax.ShapeDtypeStruct((80, SHARE), jnp.float32),
            jax.ShapeDtypeStruct((16, LANES), jnp.float32),
        ),
        in_specs=[vmem()] * 3,
        out_specs=(vmem(),) * 3,
    )(g0, g1, slots)


def quantize_kernel(g0, g1, g2, g3, d0, d1, d2, d3, maxima, gate_out, down_out, scales, gate, down, sems):
    z, x = lax.axis_index("z"), lax.axis_index("x")
    copies = []
    for s, piece in enumerate((g0, g1, g2, g3)):
        zs = (z + 4 - s) % 4
        at = pl.multiple_of((zs % 2) * 96 + (zs // 2) * 48, 16)
        copies.append(pltpu.make_async_copy(piece, gate.at[pl.ds(at, 48), :], sems.at[s]))
    for s, piece in enumerate((d0, d1, d2, d3)):
        xs = (x + 4 - s) % 4
        for h in range(2):
            at = pl.multiple_of(h * 160 + xs * 40, 8)
            copies.append(
                pltpu.make_async_copy(
                    piece.at[pl.ds(h * 40, 40), :], down.at[pl.ds(at, 40), :], sems.at[4 + 2 * s + h]
                )
            )
    for copy in copies:
        copy.start()
    lane = lax.broadcasted_iota(jnp.int32, (1, LANES), 1)
    top = jnp.max(maxima[...], axis=0) + scale_eps
    scales[...] = top

    def pick(at):
        return jnp.max(jnp.where(lane == at, top, 0.0), axis=1, keepdims=True)

    for copy in copies[:4]:
        copy.wait()
    blk = (x * 96) // BLOCK
    first = (blk + 1) * BLOCK - x * 96
    for zl in range(2):
        low, high = pick(blk + 3 * zl), pick(blk + 3 * zl + 1)
        for j in range(3):
            scale = jnp.where(j * 32 >= first, high, low)
            rows = slice(zl * 96 + j * 32, zl * 96 + j * 32 + 32)
            for k in range(GATE_BLOCKS):
                col = slice(k * BLOCK, (k + 1) * BLOCK)
                gate_out[rows, col] = (gate[rows, col] / scale[k : k + 1, :]).astype(jnp.bfloat16)
    for copy in copies[4:]:
        copy.wait()
    blk = (z * 160) // BLOCK
    first = (blk + 1) * BLOCK - z * 160
    for h in range(2):
        low, high = pick(DOWN_LANE + 5 * h + blk), pick(DOWN_LANE + 5 * h + blk + 1)
        for j in range(5):
            scale = jnp.where(j * 32 >= first, high, low)
            rows = slice(h * 160 + j * 32, h * 160 + j * 32 + 32)
            for k in range(DOWN_BLOCKS):
                col = slice(k * BLOCK, (k + 1) * BLOCK)
                down_out[rows, col] = (down[rows, col] / scale[k : k + 1, :]).astype(jnp.bfloat16)


def quantize(gates, downs, maxima):
    return pl.pallas_call(
        quantize_kernel,
        out_shape=(
            jax.ShapeDtypeStruct((192, GATE_COLS), jnp.bfloat16),
            jax.ShapeDtypeStruct((320, SHARE), jnp.bfloat16),
            jax.ShapeDtypeStruct((16, LANES), jnp.float32),
        ),
        in_specs=[anywhere()] * 8 + [vmem()],
        out_specs=(vmem(),) * 3,
        scratch_shapes=[
            pltpu.VMEM((192, GATE_COLS), jnp.float32),
            pltpu.VMEM((320, SHARE), jnp.float32),
            pltpu.SemaphoreType.DMA((12,)),
        ],
    )(*gates, *downs, maxima)


def place_kernel(g0, g1, g2, g3, d0, d1, d2, d3, gate_out, down_out, sems):
    z, x = lax.axis_index("z"), lax.axis_index("x")
    copies = []
    for s in range(4):
        xs, zs = (x + 4 - s) % 4, (z + 4 - s) % 4
        gate, down = (g0, g1, g2, g3)[s], (d0, d1, d2, d3)[s]
        for h in range(2):
            at = pl.multiple_of(h * 384 + xs * 96, 16)
            copies.append(
                pltpu.make_async_copy(
                    gate.at[pl.ds(h * 96, 96), :], gate_out.at[pl.ds(at, 96), :], sems.at[4 * s + h]
                )
            )
            at = pl.multiple_of(h * 640 + zs * 160, 16)
            copies.append(
                pltpu.make_async_copy(
                    down.at[pl.ds(h * 160, 160), :], down_out.at[pl.ds(at, 160), :], sems.at[4 * s + 2 + h]
                )
            )
    for copy in copies:
        copy.start()
    for copy in copies:
        copy.wait()


def place(gates, downs):
    return pl.pallas_call(
        place_kernel,
        out_shape=(
            jax.ShapeDtypeStruct((SHARE, GATE_COLS), jnp.bfloat16),
            jax.ShapeDtypeStruct((GATE_COLS, SHARE), jnp.bfloat16),
        ),
        in_specs=[vmem()] * 8,
        out_specs=(anywhere(),) * 2,
        scratch_shapes=[pltpu.SemaphoreType.DMA((16,))],
    )(*gates, *downs)


def gate_pairs(flip):
    pairs = []
    for yh in range(2):
        for z in range(4):
            for x in range(4):
                for yl in range(2):
                    for c in range(2):
                        target = index_of(c ^ flip, 2 * yl + z % 2, x, yh, z // 2)
                        pairs.append((index_of(yh, z, x, yl, c), target))
    return pairs


def around(array, axis):
    return [array] + [lax.ppermute(array, axis, [(i, (i + s) % 4) for i in range(4)]) for s in (1, 2, 3)]


def body(gate_param, gate_grad, gate_m, gate_v, down_param, down_grad, down_m, down_v):
    gate_new, gate_m_new, gate_v_new, down_new, down_m_new, down_v_new, slots = adam(
        (gate_param, gate_grad, gate_m, gate_v), (down_param, down_grad, down_m, down_v)
    )
    g0 = lax.ppermute(gate_new, AXES, gate_pairs(0))
    g1 = lax.ppermute(gate_new, AXES, gate_pairs(1))
    slots = lax.all_to_all(slots, ("yh", "yl", "c"), 0, 0, tiled=True)
    gate, down, maxima = partial_maxima(g0, g1, slots)
    gates = around(gate, "z")
    downs = around(down, "x")
    maxima = lax.all_to_all(
        jnp.broadcast_to(maxima[None], (16,) + maxima.shape), ("z", "x"), 0, 0, tiled=True
    )
    gate, down, scales = quantize(gates, downs, maxima)
    gate_quant, down_quant = place(around(gate, "x"), around(down, "z"))
    gate_scale = scales[:GATE_BLOCKS, :6].T
    down_scale = scales[:DOWN_BLOCKS, DOWN_LANE : DOWN_LANE + 10].T
    return (
        gate_new,
        gate_m_new,
        gate_v_new,
        down_new,
        down_m_new,
        down_v_new,
        gate_quant[None],
        gate_scale[None],
        down_quant[None],
        down_scale[None],
    )


def solution(mesh):
    parts = Mesh(mesh.devices.reshape(SIZES), AXES)
    return jax.shard_map(
        body,
        mesh=parts,
        in_specs=(P(ROWS, None),) * 8,
        out_specs=(P(ROWS, None),) * 6
        + (
            P(INST, TP, None),
            P(INST, TP, None),
            P(INST, None, TP),
            P(INST, None, TP),
        ),
        check_vma=False,
    )
```

```python
import functools

import jax
import jax.numpy as jnp
from jax import lax
from jax.experimental import pallas as pl
from jax.experimental.pallas import tpu as pltpu
from jax.sharding import Mesh, PartitionSpec as P

BLOCK = 128
LANES = 128
AXES = ("yh", "z", "x", "yl", "c")
SIZES = (2, 4, 4, 2, 2)
ROWS = ("yh", "z", "x", "yl", "c")
INST = ("yh", "z", "x")
TP = ("yl", "c")

beta_one = 0.9
beta_two = 0.999
adam_eps = 1e-08
step_rate = 0.02
decay_rate = 0.1
correct_one = 0.9999734386011124
correct_two = 0.09520785288629038
scale_eps = 1e-06

GATE_ROWS = 24
GATE_COLS = 1280
DOWN_ROWS = 10
DOWN_COLS = 3072
SHARE = 768
GATE_BLOCKS = GATE_COLS // BLOCK
DOWN_BLOCKS = SHARE // BLOCK
DOWN_LANE = 64


def index_of(yh, z, x, yl, c):
    return (((yh * 4 + z) * 4 + x) * 2 + yl) * 2 + c


def vmem():
    return pl.BlockSpec(memory_space=pltpu.VMEM)


def anywhere():
    return pl.BlockSpec(memory_space=pl.ANY)


def limit(mib):
    return pltpu.CompilerParams(vmem_limit_bytes=mib * 2**20)


def adamw_step(param, grad, moment, second):
    moment_new = beta_one * moment + (1.0 - beta_one) * grad
    second_new = beta_two * second + (1.0 - beta_two) * grad * grad
    update = moment_new / correct_one / (jnp.sqrt(second_new / correct_two) + adam_eps)
    param_new = param - step_rate * (update + decay_rate * param)
    return (param_new, moment_new, second_new)


def block_maxima(rows, first, row_count, blocks):
    size = jnp.abs(rows)
    below = lax.broadcasted_iota(jnp.int32, (row_count, 1), 0) < first
    out = []
    for part in (jnp.where(below, size, 0.0), jnp.where(below, 0.0, size)):
        top = jnp.max(part, axis=0, keepdims=True)
        tall = jnp.concatenate([top[:, k * BLOCK : (k + 1) * BLOCK] for k in range(blocks)], axis=0)
        out.append(jnp.max(tall, axis=1, keepdims=True))
    return out


def spread(low, high, blk, count, base):
    lane = lax.broadcasted_iota(jnp.int32, (1, LANES), 1) - base
    row = jnp.zeros((1, LANES), jnp.float32)
    for k in range(count):
        row = jnp.where(lane == blk * count + k, low[k : k + 1, :], row)
        row = jnp.where(lane == (blk + 1) * count + k, jnp.maximum(high[k : k + 1, :], row), row)
    return row


def adam_kernel(gp, gg, gm, gv, dp, dg, dm, dv, gpo, gmo, gvo, dpo, dmo, dvo, maxima):
    yh, z, x, yl, c = [lax.axis_index(name) for name in AXES]
    gate, gmo[...], gvo[...] = adamw_step(gp[...], gg[...], gm[...], gv[...])
    down, dmo[...], dvo[...] = adamw_step(dp[...], dg[...], dm[...], dv[...])
    gpo[...] = gate
    dpo[...] = down
    at = ((z % 2 * 4 + x) * 4 + yl * 2 + c) * GATE_ROWS
    blk = at // BLOCK
    low, high = block_maxima(gate, (blk + 1) * BLOCK - at, GATE_ROWS, GATE_BLOCKS)
    gate_row = spread(low, high, blk, GATE_BLOCKS, 0)
    at = index_of(yh, z, x, yl, c) * DOWN_ROWS
    blk = at // BLOCK
    low, high = block_maxima(down, (blk + 1) * BLOCK - at, DOWN_ROWS, 4 * DOWN_BLOCKS)
    rows = []
    for rank in range(4):
        part = slice(rank * DOWN_BLOCKS, (rank + 1) * DOWN_BLOCKS)
        row = spread(low[part], high[part], blk, DOWN_BLOCKS, DOWN_LANE)
        rows.append(jnp.where(yh * 2 + z // 2 == rank, jnp.maximum(row, gate_row), row))
    rows = jnp.concatenate(rows, axis=0)
    for i in range(16):
        maxima[i] = rows


def adam(gate, down):
    gate_shape = jax.ShapeDtypeStruct((GATE_ROWS, GATE_COLS), jnp.float32)
    down_shape = jax.ShapeDtypeStruct((DOWN_ROWS, DOWN_COLS), jnp.float32)
    return pl.pallas_call(
        adam_kernel,
        out_shape=(gate_shape,) * 3
        + (down_shape,) * 3
        + (jax.ShapeDtypeStruct((16, 4, LANES), jnp.float32),),
        in_specs=[vmem()] * 8,
        out_specs=(vmem(),) * 7,
    )(*gate, *down)


def slots_kernel(down, maxima, g0, g1, slots):
    rows = jnp.max(maxima[...], axis=0)
    for rank in range(4):
        for half in range(2):
            to = half * 4 + rank
            for k in range(DOWN_BLOCKS):
                col = slice(rank * SHARE + k * BLOCK, rank * SHARE + (k + 1) * BLOCK)
                slots[to, 8 * k : 8 * k + 8, :] = down[0:8, col]
                slots[to, 48 + 2 * k : 50 + 2 * k, :] = down[8:10, col]
            slots[to, 60:64, :] = jnp.broadcast_to(rows[rank : rank + 1], (4, LANES))


def make_slots(down, maxima, g0, g1):
    return pl.pallas_call(
        slots_kernel,
        out_shape=jax.ShapeDtypeStruct((8, 64, LANES), jnp.float32),
        in_specs=[vmem()] * 2 + [anywhere()] * 2,
        out_specs=vmem(),
        compiler_params=limit(2),
    )(down, maxima, g0, g1)


def quantize_kernel(g0, g1, slots, gate_out, down_out, scales, gate, down):
    yh, z, x = [lax.axis_index(name) for name in INST]
    gate[pl.ds(pl.multiple_of(yh * GATE_ROWS, 8), GATE_ROWS), :] = g0[...]
    gate[pl.ds(pl.multiple_of((1 - yh) * GATE_ROWS, 8), GATE_ROWS), :] = g1[...]
    for s in range(8):
        at = s * DOWN_ROWS
        for k in range(DOWN_BLOCKS):
            col = slice(k * BLOCK, (k + 1) * BLOCK)
            down[at : at + 8, col] = slots[s, 8 * k : 8 * k + 8, :]
            down[at + 8 : at + 10, col] = slots[s, 48 + 2 * k : 50 + 2 * k, :]
    lane = lax.broadcasted_iota(jnp.int32, (1, LANES), 1)
    top = jnp.max(jnp.max(slots[:, 60:64, :], axis=0), axis=0, keepdims=True) + scale_eps
    scales[...] = top

    def pick(at):
        return jnp.max(jnp.where(lane == at, top, 0.0), axis=1, keepdims=True)

    at = x * 96 + z // 2 * 48
    blk = at // BLOCK
    below = lax.broadcasted_iota(jnp.int32, (48, 1), 0) < (blk + 1) * BLOCK - at
    for k in range(GATE_BLOCKS):
        low = pick((3 * (z % 2) + blk) * GATE_BLOCKS + k)
        high = pick((3 * (z % 2) + blk + 1) * GATE_BLOCKS + k)
        col = slice(k * BLOCK, (k + 1) * BLOCK)
        gate_out[:, col] = (gate[:, col] / jnp.where(below, low, high)).astype(jnp.bfloat16)
    at = z * 160 + x * 40
    blk = at // BLOCK
    row = lax.broadcasted_iota(jnp.int32, (80, 1), 0)
    below = row % 40 < (blk + 1) * BLOCK - at
    for k in range(DOWN_BLOCKS):
        low, high = [
            jnp.where(
                row < 40,
                pick(DOWN_LANE + (blk + i) * DOWN_BLOCKS + k),
                pick(DOWN_LANE + (5 + blk + i) * DOWN_BLOCKS + k),
            )
            for i in range(2)
        ]
        col = slice(k * BLOCK, (k + 1) * BLOCK)
        down_out[:, col] = (down[:, col] / jnp.where(below, low, high)).astype(jnp.bfloat16)


def quantize(g0, g1, slots):
    return pl.pallas_call(
        quantize_kernel,
        out_shape=(
            jax.ShapeDtypeStruct((48, GATE_COLS), jnp.bfloat16),
            jax.ShapeDtypeStruct((80, SHARE), jnp.bfloat16),
            jax.ShapeDtypeStruct((1, LANES), jnp.float32),
        ),
        in_specs=[vmem()] * 3,
        out_specs=(vmem(),) * 3,
        scratch_shapes=[
            pltpu.VMEM((48, GATE_COLS), jnp.float32),
            pltpu.VMEM((80, SHARE), jnp.float32),
        ],
        compiler_params=limit(4),
    )(g0, g1, slots)


def pack_kernel(g0, g1, g2, g3, d0, d1, d2, d3, gate, down, rows):
    z, x = lax.axis_index("z"), lax.axis_index("x")
    for s, piece in enumerate((g0, g1, g2, g3)):
        zs = (z + 4 - s) % 4
        gate[pl.ds(pl.multiple_of((zs % 2) * 96 + (zs // 2) * 48, 16), 48), :] = piece[...]
    for s, piece in enumerate((d0, d1, d2, d3)):
        xs = (x + 4 - s) % 4
        wide = piece[...].astype(jnp.float32)
        for h in range(2):
            rows[pl.ds(pl.multiple_of(h * 160 + xs * 40, 8), 40), :] = wide[h * 40 : h * 40 + 40]
    down[...] = rows[...].astype(jnp.bfloat16)


def pack(gates, downs):
    return pl.pallas_call(
        pack_kernel,
        out_shape=(
            jax.ShapeDtypeStruct((192, GATE_COLS), jnp.bfloat16),
            jax.ShapeDtypeStruct((320, SHARE), jnp.bfloat16),
        ),
        in_specs=[vmem()] * 8,
        out_specs=(vmem(),) * 2,
        scratch_shapes=[pltpu.VMEM((320, SHARE), jnp.float32)],
        compiler_params=limit(6),
    )(*gates, *downs)


def place_kernel(axis, back, *refs):
    block, out, sems = refs[0], refs[-2], refs[-1]
    step = block.shape[0] // 2
    at = ((lax.axis_index(axis) + 4 - back) % 4) * step
    copies = [
        pltpu.make_async_copy(
            block.at[pl.ds(h * step, step), :],
            out.at[pl.ds(pl.multiple_of(h * 4 * step + at, 16), step), :],
            sems.at[h],
        )
        for h in range(2)
    ]
    for copy in copies:
        copy.start()
    for copy in copies:
        copy.wait()


def place(blocks, axis):
    rows, columns = blocks[0].shape
    out = ()
    for back in (0, 3, 2, 1):
        out = (
            pl.pallas_call(
                functools.partial(place_kernel, axis, back),
                out_shape=jax.ShapeDtypeStruct((rows * 4, columns), jnp.bfloat16),
                in_specs=[vmem()] + [anywhere()] * len(out),
                out_specs=anywhere(),
                input_output_aliases={1: 0} if out else {},
                scratch_shapes=[pltpu.SemaphoreType.DMA((2,))],
                compiler_params=limit(2),
            )(blocks[back], *out),
        )
    return out[0]


def gate_pairs(flip):
    pairs = []
    for yh in range(2):
        for z in range(4):
            for x in range(4):
                for yl in range(2):
                    for c in range(2):
                        target = index_of(c ^ flip, 2 * yl + z % 2, x, yh, z // 2)
                        pairs.append((index_of(yh, z, x, yl, c), target))
    return pairs


def around(array, axis):
    return [array] + [lax.ppermute(array, axis, [(i, (i + s) % 4) for i in range(4)]) for s in (1, 2, 3)]


def body(gate_param, gate_grad, gate_m, gate_v, down_param, down_grad, down_m, down_v):
    gate_new, gate_m_new, gate_v_new, down_new, down_m_new, down_v_new, maxima = adam(
        (gate_param, gate_grad, gate_m, gate_v), (down_param, down_grad, down_m, down_v)
    )
    g0 = lax.ppermute(gate_new, AXES, gate_pairs(0))
    g1 = lax.ppermute(gate_new, AXES, gate_pairs(1))
    maxima = lax.all_to_all(maxima, ("z", "x"), 0, 0, tiled=True)
    slots = make_slots(down_new, maxima, g0, g1)
    slots = lax.all_to_all(slots, ("yh", "yl", "c"), 0, 0, tiled=True)
    gate, down, scales = quantize(g0, g1, slots)
    gate, down = pack(around(gate, "z"), around(down, "x"))
    gate_quant = place(around(gate, "x"), "x")
    down_quant = place(around(down, "z"), "z")
    gate_scale = scales[0, :60].reshape(6, 10)
    down_scale = scales[0, DOWN_LANE : DOWN_LANE + 60].reshape(10, 6)
    return (
        gate_new,
        gate_m_new,
        gate_v_new,
        down_new,
        down_m_new,
        down_v_new,
        gate_quant[None],
        gate_scale[None],
        down_quant[None],
        down_scale[None],
    )


def solution(mesh):
    parts = Mesh(mesh.devices.reshape(SIZES), AXES)
    return jax.shard_map(
        body,
        mesh=parts,
        in_specs=(P(ROWS, None),) * 8,
        out_specs=(P(ROWS, None),) * 6
        + (
            P(INST, TP, None),
            P(INST, TP, None),
            P(INST, None, TP),
            P(INST, None, TP),
        ),
        check_vma=False,
    )
```

```python
import functools

import jax
import jax.numpy as jnp
from jax import lax
from jax.experimental import pallas as pl
from jax.experimental.pallas import tpu as pltpu
from jax.sharding import Mesh, PartitionSpec as P

BLOCK = 128
LANES = 128
AXES = ("yh", "z", "x", "yl", "c")
SIZES = (2, 4, 4, 2, 2)
ROWS = ("yh", "z", "x", "yl", "c")
INST = ("yh", "z", "x")
TP = ("yl", "c")

beta_one = 0.9
beta_two = 0.999
adam_eps = 1e-08
step_rate = 0.02
decay_rate = 0.1
correct_one = 0.9999734386011124
correct_two = 0.09520785288629038
scale_eps = 1e-06

GATE_ROWS = 24
GATE_COLS = 1280
DOWN_ROWS = 10
DOWN_COLS = 3072
SHARE = 768
GATE_BLOCKS = GATE_COLS // BLOCK
DOWN_BLOCKS = SHARE // BLOCK
DOWN_LANE = 64


def index_of(yh, z, x, yl, c):
    return (((yh * 4 + z) * 4 + x) * 2 + yl) * 2 + c


def vmem():
    return pl.BlockSpec(memory_space=pltpu.VMEM)


def anywhere():
    return pl.BlockSpec(memory_space=pl.ANY)


def limit(mib):
    return pltpu.CompilerParams(vmem_limit_bytes=mib * 2**20)


def adamw_step(param, grad, moment, second):
    moment_new = beta_one * moment + (1.0 - beta_one) * grad
    second_new = beta_two * second + (1.0 - beta_two) * grad * grad
    update = moment_new / correct_one / (jnp.sqrt(second_new / correct_two) + adam_eps)
    param_new = param - step_rate * (update + decay_rate * param)
    return (param_new, moment_new, second_new)


def adam_kernel(gp, gg, gm, gv, dp, dg, dm, dv, gpo, gmo, gvo, dpo, dmo, dvo, slots):
    gpo[...], gmo[...], gvo[...] = adamw_step(gp[...], gg[...], gm[...], gv[...])
    down, dmo[...], dvo[...] = adamw_step(dp[...], dg[...], dm[...], dv[...])
    dpo[...] = down
    for rank in range(4):
        for k in range(DOWN_BLOCKS):
            col = rank * SHARE + k * BLOCK
            for half in range(2):
                slots[half * 4 + rank, 8 * k : 8 * k + 8, :] = down[0:8, col : col + BLOCK]
                slots[half * 4 + rank, 48 + 2 * k : 50 + 2 * k, :] = down[8:10, col : col + BLOCK]
        for half in range(2):
            slots[half * 4 + rank, 60:64, :] = jnp.zeros((4, LANES), jnp.float32)


def adam(gate, down):
    gate_shape = jax.ShapeDtypeStruct((GATE_ROWS, GATE_COLS), jnp.float32)
    down_shape = jax.ShapeDtypeStruct((DOWN_ROWS, DOWN_COLS), jnp.float32)
    return pl.pallas_call(
        adam_kernel,
        out_shape=(gate_shape,) * 3
        + (down_shape,) * 3
        + (jax.ShapeDtypeStruct((8, 64, LANES), jnp.float32),),
        in_specs=[vmem()] * 8,
        out_specs=(vmem(),) * 7,
    )(*gate, *down)


def block_maxima(rows, first, row_count, blocks):
    size = jnp.abs(rows)
    below = lax.broadcasted_iota(jnp.int32, (row_count, 1), 0) < first
    out = []
    for part in (jnp.where(below, size, 0.0), jnp.where(below, 0.0, size)):
        top = jnp.max(part, axis=0, keepdims=True)
        tall = jnp.concatenate([top[:, k * BLOCK : (k + 1) * BLOCK] for k in range(blocks)], axis=0)
        out.append(jnp.max(tall, axis=1, keepdims=True))
    return out


def spread(low, high, blk, count, base):
    lane = lax.broadcasted_iota(jnp.int32, (1, LANES), 1) - base
    row = jnp.zeros((1, LANES), jnp.float32)
    for k in range(count):
        row = jnp.where(lane == blk * count + k, low[k : k + 1, :], row)
        row = jnp.where(lane == (blk + 1) * count + k, jnp.maximum(high[k : k + 1, :], row), row)
    return row


def unpack_kernel(g0, g1, slots, gate, down, maxima):
    yh, z, x = [lax.axis_index(name) for name in INST]
    gate[pl.ds(pl.multiple_of(yh * GATE_ROWS, 8), GATE_ROWS), :] = g0[...]
    gate[pl.ds(pl.multiple_of((1 - yh) * GATE_ROWS, 8), GATE_ROWS), :] = g1[...]
    for s in range(8):
        at = s * DOWN_ROWS
        for k in range(DOWN_BLOCKS):
            col = slice(k * BLOCK, (k + 1) * BLOCK)
            down[at : at + 8, col] = slots[s, 8 * k : 8 * k + 8, :]
            down[at + 8 : at + 10, col] = slots[s, 48 + 2 * k : 50 + 2 * k, :]
    at = x * 96 + z // 2 * 48
    blk = at // BLOCK
    low, high = block_maxima(gate[...], (blk + 1) * BLOCK - at, 48, GATE_BLOCKS)
    row = spread(low, high, 3 * (z % 2) + blk, GATE_BLOCKS, 0)
    at = z * 160 + x * 40
    blk = at // BLOCK
    for h in range(2):
        low, high = block_maxima(down[h * 40 : h * 40 + 40, :], (blk + 1) * BLOCK - at, 40, DOWN_BLOCKS)
        row = jnp.maximum(row, spread(low, high, 5 * h + blk, DOWN_BLOCKS, DOWN_LANE))
    for i in range(16):
        maxima[i] = row


def unpack(g0, g1, slots):
    return pl.pallas_call(
        unpack_kernel,
        out_shape=(
            jax.ShapeDtypeStruct((48, GATE_COLS), jnp.float32),
            jax.ShapeDtypeStruct((80, SHARE), jnp.float32),
            jax.ShapeDtypeStruct((16, 1, LANES), jnp.float32),
        ),
        in_specs=[vmem()] * 3,
        out_specs=(vmem(),) * 3,
        compiler_params=limit(4),
    )(g0, g1, slots)


def quantize_kernel(gate, down, maxima, gate_out, down_out, scales):
    yh, z, x = [lax.axis_index(name) for name in INST]
    lane = lax.broadcasted_iota(jnp.int32, (1, LANES), 1)
    top = jnp.max(maxima[...], axis=0) + scale_eps
    scales[...] = top

    def pick(at):
        return jnp.max(jnp.where(lane == at, top, 0.0), axis=1, keepdims=True)

    at = x * 96 + z // 2 * 48
    blk = at // BLOCK
    below = lax.broadcasted_iota(jnp.int32, (48, 1), 0) < (blk + 1) * BLOCK - at
    for k in range(GATE_BLOCKS):
        low = pick((3 * (z % 2) + blk) * GATE_BLOCKS + k)
        high = pick((3 * (z % 2) + blk + 1) * GATE_BLOCKS + k)
        col = slice(k * BLOCK, (k + 1) * BLOCK)
        gate_out[:, col] = (gate[:, col] / jnp.where(below, low, high)).astype(jnp.bfloat16)
    at = z * 160 + x * 40
    blk = at // BLOCK
    row = lax.broadcasted_iota(jnp.int32, (80, 1), 0)
    below = row % 40 < (blk + 1) * BLOCK - at
    for k in range(DOWN_BLOCKS):
        low, high = [
            jnp.where(
                row < 40,
                pick(DOWN_LANE + (blk + i) * DOWN_BLOCKS + k),
                pick(DOWN_LANE + (5 + blk + i) * DOWN_BLOCKS + k),
            )
            for i in range(2)
        ]
        col = slice(k * BLOCK, (k + 1) * BLOCK)
        down_out[:, col] = (down[:, col] / jnp.where(below, low, high)).astype(jnp.bfloat16)


def quantize(gate, down, maxima):
    return pl.pallas_call(
        quantize_kernel,
        out_shape=(
            jax.ShapeDtypeStruct((48, GATE_COLS), jnp.bfloat16),
            jax.ShapeDtypeStruct((80, SHARE), jnp.bfloat16),
            jax.ShapeDtypeStruct((1, LANES), jnp.float32),
        ),
        in_specs=[vmem()] * 3,
        out_specs=(vmem(),) * 3,
        compiler_params=limit(4),
    )(gate, down, maxima)


def pack_kernel(g0, g1, g2, g3, d0, d1, d2, d3, gate, down, rows):
    z, x = lax.axis_index("z"), lax.axis_index("x")
    for s, piece in enumerate((g0, g1, g2, g3)):
        zs = (z + 4 - s) % 4
        gate[pl.ds(pl.multiple_of((zs % 2) * 96 + (zs // 2) * 48, 16), 48), :] = piece[...]
    for s, piece in enumerate((d0, d1, d2, d3)):
        xs = (x + 4 - s) % 4
        wide = piece[...].astype(jnp.float32)
        for h in range(2):
            rows[pl.ds(pl.multiple_of(h * 160 + xs * 40, 8), 40), :] = wide[h * 40 : h * 40 + 40]
    down[...] = rows[...].astype(jnp.bfloat16)


def pack(gates, downs):
    return pl.pallas_call(
        pack_kernel,
        out_shape=(
            jax.ShapeDtypeStruct((192, GATE_COLS), jnp.bfloat16),
            jax.ShapeDtypeStruct((320, SHARE), jnp.bfloat16),
        ),
        in_specs=[vmem()] * 8,
        out_specs=(vmem(),) * 2,
        scratch_shapes=[pltpu.VMEM((320, SHARE), jnp.float32)],
        compiler_params=limit(6),
    )(*gates, *downs)


def place_kernel(axis, back, *refs):
    block, out, sems = refs[0], refs[-2], refs[-1]
    step = block.shape[0] // 2
    at = ((lax.axis_index(axis) + 4 - back) % 4) * step
    copies = [
        pltpu.make_async_copy(
            block.at[pl.ds(h * step, step), :],
            out.at[pl.ds(pl.multiple_of(h * 4 * step + at, 16), step), :],
            sems.at[h],
        )
        for h in range(2)
    ]
    for copy in copies:
        copy.start()
    for copy in copies:
        copy.wait()


def place(blocks, axis):
    rows, columns = blocks[0].shape
    out = ()
    for back in (0, 1, 3, 2):
        out = (
            pl.pallas_call(
                functools.partial(place_kernel, axis, back),
                out_shape=jax.ShapeDtypeStruct((rows * 4, columns), jnp.bfloat16),
                in_specs=[vmem()] + [anywhere()] * len(out),
                out_specs=anywhere(),
                input_output_aliases={1: 0} if out else {},
                scratch_shapes=[pltpu.SemaphoreType.DMA((2,))],
                compiler_params=limit(2),
            )(blocks[back], *out),
        )
    return out[0]


def gate_pairs(flip):
    pairs = []
    for yh in range(2):
        for z in range(4):
            for x in range(4):
                for yl in range(2):
                    for c in range(2):
                        target = index_of(c ^ flip, 2 * yl + z % 2, x, yh, z // 2)
                        pairs.append((index_of(yh, z, x, yl, c), target))
    return pairs


def shift(array, axis, by):
    return lax.ppermute(array, axis, [(i, (i + by) % 4) for i in range(4)])


def around(array, axis):
    return [array] + [shift(array, axis, by) for by in (1, 2, 3)]


def around_by_neighbours(array, axis):
    back = shift(array, axis, 1)
    return [array, back, shift(back, axis, 1), shift(array, axis, 3)]


def body(gate_param, gate_grad, gate_m, gate_v, down_param, down_grad, down_m, down_v):
    gate_new, gate_m_new, gate_v_new, down_new, down_m_new, down_v_new, slots = adam(
        (gate_param, gate_grad, gate_m, gate_v), (down_param, down_grad, down_m, down_v)
    )
    g0 = lax.ppermute(gate_new, AXES, gate_pairs(0))
    g1 = lax.ppermute(gate_new, AXES, gate_pairs(1))
    slots = lax.all_to_all(slots, ("yh", "yl", "c"), 0, 0, tiled=True)
    gate, down, maxima = unpack(g0, g1, slots)
    maxima = lax.all_to_all(maxima, ("z", "x"), 0, 0, tiled=True)
    gate, down, scales = quantize(gate, down, maxima)
    gate, down = pack(around(gate, "z"), around(down, "x"))
    gate_quant = place(around_by_neighbours(gate, "x"), "x")
    down_quant = place(around_by_neighbours(down, "z"), "z")
    gate_scale = scales[0, :60].reshape(6, 10)
    down_scale = scales[0, DOWN_LANE : DOWN_LANE + 60].reshape(10, 6)
    return (
        gate_new,
        gate_m_new,
        gate_v_new,
        down_new,
        down_m_new,
        down_v_new,
        gate_quant[None],
        gate_scale[None],
        down_quant[None],
        down_scale[None],
    )


def solution(mesh):
    parts = Mesh(mesh.devices.reshape(SIZES), AXES)
    return jax.shard_map(
        body,
        mesh=parts,
        in_specs=(P(ROWS, None),) * 8,
        out_specs=(P(ROWS, None),) * 6
        + (
            P(INST, TP, None),
            P(INST, TP, None),
            P(INST, None, TP),
            P(INST, None, TP),
        ),
        check_vma=False,
    )
```

```python
import functools

import jax
import jax.numpy as jnp
from jax import lax
from jax.experimental import pallas as pl
from jax.experimental.pallas import tpu as pltpu
from jax.sharding import Mesh, PartitionSpec as P

BLOCK = 128
LANES = 128
AXES = ("yh", "z", "x", "yl", "c")
SIZES = (2, 4, 4, 2, 2)
ROWS = ("yh", "z", "x", "yl", "c")
INST = ("yh", "z", "x")
TP = ("yl", "c")

beta_one = 0.9
beta_two = 0.999
adam_eps = 1e-08
step_rate = 0.02
decay_rate = 0.1
correct_one = 0.9999734386011124
correct_two = 0.09520785288629038
scale_eps = 1e-06

GATE_ROWS = 24
GATE_COLS = 1280
DOWN_ROWS = 10
DOWN_COLS = 3072
SHARE = 768
GATE_BLOCKS = GATE_COLS // BLOCK
DOWN_BLOCKS = SHARE // BLOCK
DOWN_LANE = 64


def index_of(yh, z, x, yl, c):
    return (((yh * 4 + z) * 4 + x) * 2 + yl) * 2 + c


def vmem():
    return pl.BlockSpec(memory_space=pltpu.VMEM)


def anywhere():
    return pl.BlockSpec(memory_space=pl.ANY)


def limit(mib):
    return pltpu.CompilerParams(vmem_limit_bytes=mib * 2**20)


def adamw_step(param, grad, moment, second):
    moment_new = beta_one * moment + (1.0 - beta_one) * grad
    second_new = beta_two * second + (1.0 - beta_two) * grad * grad
    update = moment_new / correct_one / (jnp.sqrt(second_new / correct_two) + adam_eps)
    param_new = param - step_rate * (update + decay_rate * param)
    return (param_new, moment_new, second_new)


def block_maxima(rows, first, row_count, blocks):
    size = jnp.abs(rows)
    below = lax.broadcasted_iota(jnp.int32, (row_count, 1), 0) < first
    out = []
    for part in (jnp.where(below, size, 0.0), jnp.where(below, 0.0, size)):
        top = jnp.max(part, axis=0, keepdims=True)
        tall = jnp.concatenate([top[:, k * BLOCK : (k + 1) * BLOCK] for k in range(blocks)], axis=0)
        out.append(jnp.max(tall, axis=1, keepdims=True))
    return out


def spread(low, high, blk, count, base):
    lane = lax.broadcasted_iota(jnp.int32, (1, LANES), 1) - base
    row = jnp.zeros((1, LANES), jnp.float32)
    for k in range(count):
        row = jnp.where(lane == blk * count + k, low[k : k + 1, :], row)
        row = jnp.where(lane == (blk + 1) * count + k, jnp.maximum(high[k : k + 1, :], row), row)
    return row


def adam_kernel(gp, gg, gm, gv, dp, dg, dm, dv, gpo, gmo, gvo, dpo, dmo, dvo, slots):
    _, z, x, yl, c = [lax.axis_index(name) for name in AXES]
    gate, gmo[...], gvo[...] = adamw_step(gp[...], gg[...], gm[...], gv[...])
    down, dmo[...], dvo[...] = adamw_step(dp[...], dg[...], dm[...], dv[...])
    gpo[...] = gate
    dpo[...] = down
    at = ((z % 2 * 4 + x) * 4 + yl * 2 + c) * GATE_ROWS
    blk = at // BLOCK
    low, high = block_maxima(gate, (blk + 1) * BLOCK - at, GATE_ROWS, GATE_BLOCKS)
    row = spread(low, high, blk, GATE_BLOCKS, 0)
    for rank in range(4):
        for half in range(2):
            to = half * 4 + rank
            for k in range(DOWN_BLOCKS):
                col = slice(rank * SHARE + k * BLOCK, rank * SHARE + (k + 1) * BLOCK)
                slots[to, 8 * k : 8 * k + 8, :] = down[0:8, col]
                slots[to, 48 + 2 * k : 50 + 2 * k, :] = down[8:10, col]
            slots[to, 60:64, :] = jnp.broadcast_to(row, (4, LANES))


def adam(gate, down):
    gate_shape = jax.ShapeDtypeStruct((GATE_ROWS, GATE_COLS), jnp.float32)
    down_shape = jax.ShapeDtypeStruct((DOWN_ROWS, DOWN_COLS), jnp.float32)
    return pl.pallas_call(
        adam_kernel,
        out_shape=(gate_shape,) * 3
        + (down_shape,) * 3
        + (jax.ShapeDtypeStruct((8, 64, LANES), jnp.float32),),
        in_specs=[vmem()] * 8,
        out_specs=(vmem(),) * 7,
    )(*gate, *down)


def unpack_kernel(slots, down, maxima):
    _, z, x, _, _ = [lax.axis_index(name) for name in AXES]
    for s in range(8):
        at = s * DOWN_ROWS
        for k in range(DOWN_BLOCKS):
            col = slice(k * BLOCK, (k + 1) * BLOCK)
            down[at : at + 8, col] = slots[s, 8 * k : 8 * k + 8, :]
            down[at + 8 : at + 10, col] = slots[s, 48 + 2 * k : 50 + 2 * k, :]
    halves = [jnp.max(jnp.max(slots[4 * h : 4 * h + 4, 60:64, :], axis=0), axis=0, keepdims=True) for h in range(2)]
    at = z * 160 + x * 40
    blk = at // BLOCK
    for h in range(2):
        low, high = block_maxima(down[h * 40 : h * 40 + 40, :], (blk + 1) * BLOCK - at, 40, DOWN_BLOCKS)
        halves[0] = jnp.maximum(halves[0], spread(low, high, 5 * h + blk, DOWN_BLOCKS, DOWN_LANE))
    rows = jnp.concatenate(halves + halves, axis=0)
    for i in range(16):
        maxima[i] = rows


def unpack(slots):
    return pl.pallas_call(
        unpack_kernel,
        out_shape=(
            jax.ShapeDtypeStruct((80, SHARE), jnp.float32),
            jax.ShapeDtypeStruct((16, 4, LANES), jnp.float32),
        ),
        in_specs=[vmem()],
        out_specs=(vmem(),) * 2,
        compiler_params=limit(4),
    )(slots)


def quantize_kernel(g0, g1, down, maxima, gate_out, down_out, scales, gate):
    yh, z, x, yl, c = [lax.axis_index(name) for name in AXES]
    gate[pl.ds(pl.multiple_of(yh * GATE_ROWS, 8), GATE_ROWS), :] = g0[...]
    gate[pl.ds(pl.multiple_of((1 - yh) * GATE_ROWS, 8), GATE_ROWS), :] = g1[...]
    lane = lax.broadcasted_iota(jnp.int32, (1, LANES), 1)
    by_core = [jnp.max(maxima[8 * i : 8 * i + 8], axis=0) for i in range(2)]
    rows = jnp.where(c == 0, by_core[0], by_core[1])
    gate_row = jnp.where(yl == 0, rows[0:1, :], rows[1:2, :])
    down_row = jnp.maximum(by_core[0], by_core[1])[0:1, :]
    top = jnp.where(lane < DOWN_LANE, gate_row, down_row) + scale_eps
    scales[...] = top

    def pick(at):
        return jnp.max(jnp.where(lane == at, top, 0.0), axis=1, keepdims=True)

    at = x * 96 + z // 2 * 48
    blk = at // BLOCK
    below = lax.broadcasted_iota(jnp.int32, (48, 1), 0) < (blk + 1) * BLOCK - at
    for k in range(GATE_BLOCKS):
        low = pick((3 * (z % 2) + blk) * GATE_BLOCKS + k)
        high = pick((3 * (z % 2) + blk + 1) * GATE_BLOCKS + k)
        col = slice(k * BLOCK, (k + 1) * BLOCK)
        gate_out[:, col] = (gate[:, col] / jnp.where(below, low, high)).astype(jnp.bfloat16)
    at = z * 160 + x * 40
    blk = at // BLOCK
    row = lax.broadcasted_iota(jnp.int32, (80, 1), 0)
    below = row % 40 < (blk + 1) * BLOCK - at
    for k in range(DOWN_BLOCKS):
        low, high = [
            jnp.where(
                row < 40,
                pick(DOWN_LANE + (blk + i) * DOWN_BLOCKS + k),
                pick(DOWN_LANE + (5 + blk + i) * DOWN_BLOCKS + k),
            )
            for i in range(2)
        ]
        col = slice(k * BLOCK, (k + 1) * BLOCK)
        down_out[:, col] = (down[:, col] / jnp.where(below, low, high)).astype(jnp.bfloat16)


def quantize(g0, g1, down, maxima):
    return pl.pallas_call(
        quantize_kernel,
        out_shape=(
            jax.ShapeDtypeStruct((48, GATE_COLS), jnp.bfloat16),
            jax.ShapeDtypeStruct((80, SHARE), jnp.bfloat16),
            jax.ShapeDtypeStruct((1, LANES), jnp.float32),
        ),
        in_specs=[vmem()] * 4,
        out_specs=(vmem(),) * 3,
        scratch_shapes=[pltpu.VMEM((48, GATE_COLS), jnp.float32)],
        compiler_params=limit(4),
    )(g0, g1, down, maxima)


def pack_kernel(g0, g1, g2, g3, d0, d1, d2, d3, gate, down, rows):
    z, x = lax.axis_index("z"), lax.axis_index("x")
    for s, piece in enumerate((g0, g1, g2, g3)):
        zs = (z + 4 - s) % 4
        gate[pl.ds(pl.multiple_of((zs % 2) * 96 + (zs // 2) * 48, 16), 48), :] = piece[...]
    for s, piece in enumerate((d0, d1, d2, d3)):
        xs = (x + 4 - s) % 4
        wide = piece[...].astype(jnp.float32)
        for h in range(2):
            rows[pl.ds(pl.multiple_of(h * 160 + xs * 40, 8), 40), :] = wide[h * 40 : h * 40 + 40]
    down[...] = rows[...].astype(jnp.bfloat16)


def pack(gates, downs):
    return pl.pallas_call(
        pack_kernel,
        out_shape=(
            jax.ShapeDtypeStruct((192, GATE_COLS), jnp.bfloat16),
            jax.ShapeDtypeStruct((320, SHARE), jnp.bfloat16),
        ),
        in_specs=[vmem()] * 8,
        out_specs=(vmem(),) * 2,
        scratch_shapes=[pltpu.VMEM((320, SHARE), jnp.float32)],
        compiler_params=limit(6),
    )(*gates, *downs)


def place_kernel(axis, back, *refs):
    block, out, sems = refs[0], refs[-2], refs[-1]
    step = block.shape[0] // 2
    at = ((lax.axis_index(axis) + 4 - back) % 4) * step
    copies = [
        pltpu.make_async_copy(
            block.at[pl.ds(h * step, step), :],
            out.at[pl.ds(pl.multiple_of(h * 4 * step + at, 16), step), :],
            sems.at[h],
        )
        for h in range(2)
    ]
    for copy in copies:
        copy.start()
    for copy in copies:
        copy.wait()


def place(blocks, axis):
    rows, columns = blocks[0].shape
    out = ()
    for back in (0, 1, 3, 2):
        out = (
            pl.pallas_call(
                functools.partial(place_kernel, axis, back),
                out_shape=jax.ShapeDtypeStruct((rows * 4, columns), jnp.bfloat16),
                in_specs=[vmem()] + [anywhere()] * len(out),
                out_specs=anywhere(),
                input_output_aliases={1: 0} if out else {},
                scratch_shapes=[pltpu.SemaphoreType.DMA((2,))],
                compiler_params=limit(2),
            )(blocks[back], *out),
        )
    return out[0]


def gate_pairs(flip):
    pairs = []
    for yh in range(2):
        for z in range(4):
            for x in range(4):
                for yl in range(2):
                    for c in range(2):
                        target = index_of(c ^ flip, 2 * yl + z % 2, x, yh, z // 2)
                        pairs.append((index_of(yh, z, x, yl, c), target))
    return pairs


def shift(array, axis, by):
    return lax.ppermute(array, axis, [(i, (i + by) % 4) for i in range(4)])


def around(array, axis):
    return [array] + [shift(array, axis, by) for by in (1, 2, 3)]


def around_by_neighbours(array, axis):
    back = shift(array, axis, 1)
    return [array, back, shift(back, axis, 1), shift(array, axis, 3)]


def body(gate_param, gate_grad, gate_m, gate_v, down_param, down_grad, down_m, down_v):
    gate_new, gate_m_new, gate_v_new, down_new, down_m_new, down_v_new, slots = adam(
        (gate_param, gate_grad, gate_m, gate_v), (down_param, down_grad, down_m, down_v)
    )
    g0 = lax.ppermute(gate_new, AXES, gate_pairs(0))
    g1 = lax.ppermute(gate_new, AXES, gate_pairs(1))
    slots = lax.all_to_all(slots, ("yh", "yl", "c"), 0, 0, tiled=True)
    down, maxima = unpack(slots)
    maxima = lax.all_to_all(maxima, ("z", "x"), 0, 0, tiled=True)
    gate, down, scales = quantize(g0, g1, down, maxima)
    gate, down = pack(around(gate, "z"), around(down, "x"))
    gate_quant = place(around_by_neighbours(gate, "x"), "x")
    down_quant = place(around_by_neighbours(down, "z"), "z")
    gate_scale = scales[0, :60].reshape(6, 10)
    down_scale = scales[0, DOWN_LANE : DOWN_LANE + 60].reshape(10, 6)
    return (
        gate_new,
        gate_m_new,
        gate_v_new,
        down_new,
        down_m_new,
        down_v_new,
        gate_quant[None],
        gate_scale[None],
        down_quant[None],
        down_scale[None],
    )


def solution(mesh):
    parts = Mesh(mesh.devices.reshape(SIZES), AXES)
    return jax.shard_map(
        body,
        mesh=parts,
        in_specs=(P(ROWS, None),) * 8,
        out_specs=(P(ROWS, None),) * 6
        + (
            P(INST, TP, None),
            P(INST, TP, None),
            P(INST, None, TP),
            P(INST, None, TP),
        ),
        check_vma=False,
    )
```

```python
import functools

import jax
import jax.numpy as jnp
from jax import lax
from jax.experimental import pallas as pl
from jax.experimental.pallas import tpu as pltpu
from jax.sharding import Mesh, PartitionSpec as P

BLOCK = 128
LANES = 128
AXES = ("yh", "z", "x", "yl", "c")
SIZES = (2, 4, 4, 2, 2)
ROWS = ("yh", "z", "x", "yl", "c")
INST = ("yh", "z", "x")
TP = ("yl", "c")

beta_one = 0.9
beta_two = 0.999
adam_eps = 1e-08
step_rate = 0.02
decay_rate = 0.1
correct_one = 0.9999734386011124
correct_two = 0.09520785288629038
scale_eps = 1e-06

GATE_ROWS = 24
GATE_COLS = 1280
DOWN_ROWS = 10
DOWN_COLS = 3072
SHARE = 768
GATE_BLOCKS = GATE_COLS // BLOCK
DOWN_BLOCKS = SHARE // BLOCK
DOWN_LANE = 64


def index_of(yh, z, x, yl, c):
    return (((yh * 4 + z) * 4 + x) * 2 + yl) * 2 + c


def vmem():
    return pl.BlockSpec(memory_space=pltpu.VMEM)


def anywhere():
    return pl.BlockSpec(memory_space=pl.ANY)


def limit(mib):
    return pltpu.CompilerParams(vmem_limit_bytes=mib * 2**20)


def adamw_step(param, grad, moment, second):
    moment_new = beta_one * moment + (1.0 - beta_one) * grad
    second_new = beta_two * second + (1.0 - beta_two) * grad * grad
    update = moment_new / correct_one / (jnp.sqrt(second_new / correct_two) + adam_eps)
    param_new = param - step_rate * (update + decay_rate * param)
    return (param_new, moment_new, second_new)


def block_maxima(rows, first, row_count, blocks):
    size = jnp.abs(rows)
    below = lax.broadcasted_iota(jnp.int32, (row_count, 1), 0) < first
    out = []
    for part in (jnp.where(below, size, 0.0), jnp.where(below, 0.0, size)):
        top = jnp.max(part, axis=0, keepdims=True)
        tall = jnp.concatenate([top[:, k * BLOCK : (k + 1) * BLOCK] for k in range(blocks)], axis=0)
        out.append(jnp.max(tall, axis=1, keepdims=True))
    return out


def spread(low, high, blk, count, base):
    lane = lax.broadcasted_iota(jnp.int32, (count, LANES), 1) - base
    first = blk * count + lax.broadcasted_iota(jnp.int32, (count, LANES), 0)
    both = jnp.where(lane == first, low, 0.0) + jnp.where(lane == first + count, high, 0.0)
    return jnp.max(both, axis=0, keepdims=True)


def adam_kernel(gp, gg, gm, gv, dp, dg, dm, dv, gpo, gmo, gvo, dpo, dmo, dvo, slots):
    _, z, x, yl, c = [lax.axis_index(name) for name in AXES]
    gate, gmo[...], gvo[...] = adamw_step(gp[...], gg[...], gm[...], gv[...])
    down, dmo[...], dvo[...] = adamw_step(dp[...], dg[...], dm[...], dv[...])
    gpo[...] = gate
    dpo[...] = down
    at = ((z % 2 * 4 + x) * 4 + yl * 2 + c) * GATE_ROWS
    blk = at // BLOCK
    low, high = block_maxima(gate, (blk + 1) * BLOCK - at, GATE_ROWS, GATE_BLOCKS)
    row = spread(low, high, blk, GATE_BLOCKS, 0)
    for rank in range(4):
        for half in range(2):
            to = half * 4 + rank
            for k in range(DOWN_BLOCKS):
                col = slice(rank * SHARE + k * BLOCK, rank * SHARE + (k + 1) * BLOCK)
                slots[to, 8 * k : 8 * k + 8, :] = down[0:8, col]
                slots[to, 48 + 2 * k : 50 + 2 * k, :] = down[8:10, col]
            slots[to, 60:64, :] = jnp.broadcast_to(row, (4, LANES))


def adam(gate, down):
    gate_shape = jax.ShapeDtypeStruct((GATE_ROWS, GATE_COLS), jnp.float32)
    down_shape = jax.ShapeDtypeStruct((DOWN_ROWS, DOWN_COLS), jnp.float32)
    return pl.pallas_call(
        adam_kernel,
        out_shape=(gate_shape,) * 3
        + (down_shape,) * 3
        + (jax.ShapeDtypeStruct((8, 64, LANES), jnp.float32),),
        in_specs=[vmem()] * 8,
        out_specs=(vmem(),) * 7,
    )(*gate, *down)


def unpack_kernel(slots, down, maxima):
    _, z, x, _, _ = [lax.axis_index(name) for name in AXES]
    for s in range(8):
        at = s * DOWN_ROWS
        for k in range(DOWN_BLOCKS):
            col = slice(k * BLOCK, (k + 1) * BLOCK)
            down[at : at + 8, col] = slots[s, 8 * k : 8 * k + 8, :]
            down[at + 8 : at + 10, col] = slots[s, 48 + 2 * k : 50 + 2 * k, :]
    halves = [jnp.max(jnp.max(slots[4 * h : 4 * h + 4, 60:64, :], axis=0), axis=0, keepdims=True) for h in range(2)]
    at = z * 160 + x * 40
    blk = at // BLOCK
    for h in range(2):
        low, high = block_maxima(down[h * 40 : h * 40 + 40, :], (blk + 1) * BLOCK - at, 40, DOWN_BLOCKS)
        halves[0] = jnp.maximum(halves[0], spread(low, high, 5 * h + blk, DOWN_BLOCKS, DOWN_LANE))
    rows = jnp.concatenate(halves, axis=0)
    for i in range(16):
        maxima[i] = rows


def unpack(slots):
    return pl.pallas_call(
        unpack_kernel,
        out_shape=(
            jax.ShapeDtypeStruct((80, SHARE), jnp.float32),
            jax.ShapeDtypeStruct((16, 2, LANES), jnp.float32),
        ),
        in_specs=[vmem()],
        out_specs=(vmem(),) * 2,
        compiler_params=limit(4),
    )(slots)


def quantize_kernel(g0, g1, down, maxima, gate_out, down_out, scales, gate):
    yh, z, x, yl, c = [lax.axis_index(name) for name in AXES]
    gate[pl.ds(pl.multiple_of(yh * GATE_ROWS, 8), GATE_ROWS), :] = g0[...]
    gate[pl.ds(pl.multiple_of((1 - yh) * GATE_ROWS, 8), GATE_ROWS), :] = g1[...]
    lane = lax.broadcasted_iota(jnp.int32, (1, LANES), 1)
    by_core = [jnp.max(maxima[8 * i : 8 * i + 8], axis=0) for i in range(2)]
    rows = jnp.where(c == 0, by_core[0], by_core[1])
    gate_row = jnp.where(yl == 0, rows[0:1, :], rows[1:2, :])
    down_row = jnp.maximum(by_core[0], by_core[1])[0:1, :]
    top = jnp.where(lane < DOWN_LANE, gate_row, down_row) + scale_eps
    scales[...] = top

    def pick(at):
        return jnp.max(jnp.where(lane == at, top, 0.0), axis=1, keepdims=True)

    at = x * 96 + z // 2 * 48
    blk = at // BLOCK
    below = lax.broadcasted_iota(jnp.int32, (48, 1), 0) < (blk + 1) * BLOCK - at
    for k in range(GATE_BLOCKS):
        low = pick((3 * (z % 2) + blk) * GATE_BLOCKS + k)
        high = pick((3 * (z % 2) + blk + 1) * GATE_BLOCKS + k)
        col = slice(k * BLOCK, (k + 1) * BLOCK)
        gate_out[:, col] = (gate[:, col] / jnp.where(below, low, high)).astype(jnp.bfloat16)
    at = z * 160 + x * 40
    blk = at // BLOCK
    row = lax.broadcasted_iota(jnp.int32, (80, 1), 0)
    below = row % 40 < (blk + 1) * BLOCK - at
    for k in range(DOWN_BLOCKS):
        low, high = [
            jnp.where(
                row < 40,
                pick(DOWN_LANE + (blk + i) * DOWN_BLOCKS + k),
                pick(DOWN_LANE + (5 + blk + i) * DOWN_BLOCKS + k),
            )
            for i in range(2)
        ]
        col = slice(k * BLOCK, (k + 1) * BLOCK)
        down_out[:, col] = (down[:, col] / jnp.where(below, low, high)).astype(jnp.bfloat16)


def quantize(g0, g1, down, maxima):
    return pl.pallas_call(
        quantize_kernel,
        out_shape=(
            jax.ShapeDtypeStruct((48, GATE_COLS), jnp.bfloat16),
            jax.ShapeDtypeStruct((80, SHARE), jnp.bfloat16),
            jax.ShapeDtypeStruct((1, LANES), jnp.float32),
        ),
        in_specs=[vmem()] * 4,
        out_specs=(vmem(),) * 3,
        scratch_shapes=[pltpu.VMEM((48, GATE_COLS), jnp.float32)],
        compiler_params=limit(4),
    )(g0, g1, down, maxima)


def pack_kernel(g0, g1, g2, g3, d0, d1, d2, d3, gate, down, rows):
    z, x = lax.axis_index("z"), lax.axis_index("x")
    for s, piece in enumerate((g0, g1, g2, g3)):
        zs = (z + 4 - s) % 4
        gate[pl.ds(pl.multiple_of((zs % 2) * 96 + (zs // 2) * 48, 16), 48), :] = piece[...]
    for s, piece in enumerate((d0, d1, d2, d3)):
        xs = (x + 4 - s) % 4
        wide = piece[...].astype(jnp.float32)
        for h in range(2):
            rows[pl.ds(pl.multiple_of(h * 160 + xs * 40, 8), 40), :] = wide[h * 40 : h * 40 + 40]
    down[...] = rows[...].astype(jnp.bfloat16)


def pack(gates, downs):
    return pl.pallas_call(
        pack_kernel,
        out_shape=(
            jax.ShapeDtypeStruct((192, GATE_COLS), jnp.bfloat16),
            jax.ShapeDtypeStruct((320, SHARE), jnp.bfloat16),
        ),
        in_specs=[vmem()] * 8,
        out_specs=(vmem(),) * 2,
        scratch_shapes=[pltpu.VMEM((320, SHARE), jnp.float32)],
        compiler_params=limit(6),
    )(*gates, *downs)


def place_kernel(axis, back, *refs):
    block, out, sems = refs[0], refs[-2], refs[-1]
    step = block.shape[0] // 2
    at = ((lax.axis_index(axis) + 4 - back) % 4) * step
    copies = [
        pltpu.make_async_copy(
            block.at[pl.ds(h * step, step), :],
            out.at[pl.ds(pl.multiple_of(h * 4 * step + at, 16), step), :],
            sems.at[h],
        )
        for h in range(2)
    ]
    for copy in copies:
        copy.start()
    for copy in copies:
        copy.wait()


def place(blocks, axis):
    rows, columns = blocks[0].shape
    out = ()
    for back in (0, 1, 3, 2):
        out = (
            pl.pallas_call(
                functools.partial(place_kernel, axis, back),
                out_shape=jax.ShapeDtypeStruct((rows * 4, columns), jnp.bfloat16),
                in_specs=[vmem()] + [anywhere()] * len(out),
                out_specs=anywhere(),
                input_output_aliases={1: 0} if out else {},
                scratch_shapes=[pltpu.SemaphoreType.DMA((2,))],
                compiler_params=limit(2),
            )(blocks[back], *out),
        )
    return out[0]


def gate_pairs(flip):
    pairs = []
    for yh in range(2):
        for z in range(4):
            for x in range(4):
                for yl in range(2):
                    for c in range(2):
                        target = index_of(c ^ flip, 2 * yl + z % 2, x, yh, z // 2)
                        pairs.append((index_of(yh, z, x, yl, c), target))
    return pairs


def shift(array, axis, by):
    return lax.ppermute(array, axis, [(i, (i + by) % 4) for i in range(4)])


def around(array, axis, order):
    moved = {by: shift(array, axis, by) for by in order}
    return [array] + [moved[by] for by in (1, 2, 3)]


def around_by_neighbours(array, axis, way):
    near = {by: shift(array, axis, by) for by in (way, 4 - way)}
    return [array, near[1], shift(near[way], axis, way), near[3]]


def body(gate_param, gate_grad, gate_m, gate_v, down_param, down_grad, down_m, down_v):
    gate_new, gate_m_new, gate_v_new, down_new, down_m_new, down_v_new, slots = adam(
        (gate_param, gate_grad, gate_m, gate_v), (down_param, down_grad, down_m, down_v)
    )
    g0 = lax.ppermute(gate_new, AXES, gate_pairs(0))
    g1 = lax.ppermute(gate_new, AXES, gate_pairs(1))
    slots = lax.all_to_all(slots, ("yh", "yl", "c"), 0, 0, tiled=True)
    down, maxima = unpack(slots)
    maxima = lax.all_to_all(maxima, ("z", "x"), 0, 0, tiled=True)
    gate, down, scales = quantize(g0, g1, down, maxima)
    gate, down = pack(around(gate, "z", (1, 2, 3)), around(down, "x", (2, 1, 3)))
    gate_quant = place(around_by_neighbours(gate, "x", 1), "x")
    down_quant = place(around_by_neighbours(down, "z", 3), "z")
    gate_scale = scales[0, :60].reshape(6, 10)
    down_scale = scales[0, DOWN_LANE : DOWN_LANE + 60].reshape(10, 6)
    return (
        gate_new,
        gate_m_new,
        gate_v_new,
        down_new,
        down_m_new,
        down_v_new,
        gate_quant[None],
        gate_scale[None],
        down_quant[None],
        down_scale[None],
    )


def solution(mesh):
    parts = Mesh(mesh.devices.reshape(SIZES), AXES)
    return jax.shard_map(
        body,
        mesh=parts,
        in_specs=(P(ROWS, None),) * 8,
        out_specs=(P(ROWS, None),) * 6
        + (
            P(INST, TP, None),
            P(INST, TP, None),
            P(INST, None, TP),
            P(INST, None, TP),
        ),
        check_vma=False,
    )
```
